32 devices in a mesh: space: 8 (over z, y), chan: 4 (over x, core).
Axes of the slice: x: 2, y: 2, z: 4, core: 2. Of those that a mesh axis runs over, the one named last changes fastest.
Arguments:
- latent: bfloat16 [1, 8, 160, 512], P(None, 'space', None, 'chan'), may hold values from -12 to 12
- cache_mid: bfloat16 [2, 8, 160, 512], P(None, 'space', None, 'chan'), may hold values from -6 to 6
- norm1_gain: float32 [512], P('chan'), may hold values from 0.1 to 1.9
- norm1_bias: float32 [512], P('chan'), may hold values from -3 to 3
- conv1_weight: bfloat16 [3, 3, 3, 512, 512], P(None, None, None, 'chan'), may hold values from -0.0625 to 0.0625
- conv1_bias: float32 [512], P('chan'), may hold values from -2 to 2
- cache_up: bfloat16 [2, 16, 320, 512], P(None, 'space', 'chan'), may hold values from -6 to 6
- norm2_gain: float32 [512], replicated, may hold values from 0.1 to 1.9
- norm2_bias: float32 [512], replicated, may hold values from -3 to 3
- conv2_weight: bfloat16 [3, 3, 3, 512, 512], P(None, None, None, None, 'chan'), may hold values from -0.0546875 to 0.0546875
- conv2_bias: float32 [512], replicated, may hold values from -2 to 2
Outputs:
- up_features: bfloat16 [1, 16, 320, 512], P(None, 'space', 'chan')
The draws below stay inside these ranges and needn't reach their ends.
All inputs are finite; a program needn't handle non-finite values.
Results may differ from the reference program's by a relative error of at most 0.0038.
The reference program's roundings to bfloat16 on the way (of `normed_mid`, `merged`, `upsampled` and `normed_up`) count: a program that leaves them out, or rounds other values in their place, can miss the bound.
Values may be sent and summed in bfloat16 or wider, within the bound.
A program may use at most 64 MiB of HBM per device.

```python
import jax
import jax.numpy as jnp
from jax import lax

CH = 512
GROUPS = 32
FRAMES = 1
W = 160
GS = 16
H = 8
H2 = 16
W2 = 320


def draw_latent(key, part):
    first_key, second_key, rough_key, offset_key = jax.random.split(key, 4)
    row_place = jnp.arange(H, dtype=jnp.float32) / max(H - 1, 1)
    row_rough = jnp.exp(jax.random.uniform(rough_key, (H,), jnp.float32, -1.0, 1.0))
    base = jax.random.normal(first_key, (FRAMES, H, W, CH), jnp.float32)
    row_scale = 0.4 * 3.0 ** row_place * row_rough
    row_offset = jax.random.uniform(offset_key, (H,), jnp.float32, -1.5, 1.5)
    chan_scale = jnp.exp(jax.random.uniform(second_key, (CH,), jnp.float32, -0.7, 0.7))
    drawn = base * row_scale[None, :, None, None] * chan_scale + row_offset[None, :, None, None]
    return jnp.clip(drawn, -12.0, 12.0).astype(jnp.bfloat16)


def with_spikes(entries, key, source, target, parts, factor):
    owner, partner = [(jnp.arange(entries.shape[axis_at]) // (entries.shape[axis_at] // parts)).reshape([-1 if axis == axis_at else 1 for axis in range(entries.ndim)]) for axis_at in (source, target)]
    chosen = jax.random.permutation(key, parts)[partner]
    strong = (owner == chosen) | (owner == (partner + parts // 2) % parts)
    return jnp.where(strong, factor * entries, entries)


def block_scale(key, dims, cuts, smallest, high):
    def one(position, blocks):
        steps = jax.random.uniform(jax.random.fold_in(jax.random.fold_in(key, 6), position), (blocks,), jnp.float32, smallest / len(cuts), high / len(cuts))
        return jnp.repeat(jnp.exp(steps), dims[position] // blocks).reshape((-1,) + (1,) * (len(dims) - position - 1))

    loudness = one(*cuts[0])
    for cut in cuts[1:]:
        loudness = loudness * one(*cut)
    return loudness


def normal_values(own_key, shape, spread, reach, shards=(), held_as=jnp.bfloat16):
    values = spread * jax.random.normal(own_key, shape, jnp.float32)
    if shards:
        values = values * block_scale(own_key, shape, shards, -0.22, 0.18)
    return jnp.clip(values, -reach, reach).astype(held_as)


def noise_with(own_key, dims, width, bound, pieces, heavy, kind=jnp.bfloat16):
    values = width * jax.random.normal(own_key, dims, jnp.float32)
    if pieces:
        values = values * block_scale(own_key, dims, pieces, -0.22, 0.18)
    return jnp.clip(with_spikes(values, jax.random.fold_in(own_key, 3), *heavy), -bound, bound).astype(kind)


def setup_inputs(seed: int = 0) -> dict:
    keys = jax.random.split(jax.random.key(seed), 12)
    latent = draw_latent(jax.random.fold_in(keys[11], 71), 0)
    cache_mid = normal_values(keys[1], (2, H, W, CH), 1.0, 6.0, ((1, 8), (3, 4)))
    norm1_gain = jnp.clip(1.0 + 0.18 * jax.random.normal(keys[2], (CH,), jnp.float32), 0.1, 1.9)
    norm1_bias = normal_values(keys[3], (CH,), 0.5, 3.0, ((0, 4),), jnp.float32)
    conv1_weight = noise_with(keys[4], (3, 3, 3, CH, CH), (27 * CH) ** -0.5, 0.0625, ((3, 4),), (3, 4, 4, 2.0))
    conv1_bias = normal_values(keys[5], (CH,), 0.3, 2.0, ((0, 4),), jnp.float32)
    cache_up = normal_values(keys[6], (2, H2, W2, CH), 1.0, 6.0, ((1, 8), (2, 4)))
    norm2_gain = jnp.clip(1.0 + 0.18 * jax.random.normal(keys[7], (CH,), jnp.float32), 0.1, 1.9)
    norm2_bias = normal_values(keys[8], (CH,), 0.5, 3.0, (), jnp.float32)
    conv2_weight = normal_values(keys[9], (3, 3, 3, CH, CH), (27 * CH) ** -0.5, 0.0546875, ((4, 4),))
    conv2_bias = normal_values(keys[10], (CH,), 0.3, 2.0, (), jnp.float32)
    return dict(latent=latent, cache_mid=cache_mid, norm1_gain=norm1_gain, norm1_bias=norm1_bias, conv1_weight=conv1_weight, conv1_bias=conv1_bias, cache_up=cache_up, norm2_gain=norm2_gain, norm2_bias=norm2_bias, conv2_weight=conv2_weight, conv2_bias=conv2_bias)


epsilon = 1e-06

def norm_silu(values, gain, bias):
    layout_shape = values.shape
    grouped = values.reshape(layout_shape[:-1] + (GROUPS, GS))
    group_mean = lax.optimization_barrier(jnp.mean(grouped, axis=(0, 1, 2, 4), keepdims=True))
    centred = grouped - group_mean
    group_var = lax.optimization_barrier(jnp.mean(centred * centred, axis=(0, 1, 2, 4), keepdims=True))
    scaled = (centred * lax.rsqrt(group_var + epsilon)).reshape(layout_shape)
    return jax.nn.silu(scaled * gain + bias)

def causal_conv(sequence, kernel):
    result = lax.conv_general_dilated(sequence.astype(jnp.float32)[None], kernel.astype(jnp.float32), (1, 1, 1), ((0, 0), (1, 1), (1, 1)), dimension_numbers=('NDHWC', 'DHWIO', 'NDHWC'), precision=lax.Precision.HIGHEST)
    return result[0]

def reference(latent, cache_mid, norm1_gain, norm1_bias, conv1_weight, conv1_bias, cache_up, norm2_gain, norm2_bias, conv2_weight, conv2_bias):
    values = latent.astype(jnp.float32)
    normed_mid = norm_silu(values, norm1_gain, norm1_bias).astype(jnp.bfloat16)
    conv_mid = causal_conv(jnp.concatenate([cache_mid, normed_mid], axis=0), conv1_weight)
    merged = (values + conv_mid + conv1_bias).astype(jnp.bfloat16)
    upsampled = jnp.repeat(jnp.repeat(merged, 2, axis=1), 2, axis=2)
    normed_up = norm_silu(upsampled.astype(jnp.float32), norm2_gain, norm2_bias).astype(jnp.bfloat16)
    up_conv = causal_conv(jnp.concatenate([cache_up, normed_up], axis=0), conv2_weight)
    return (up_conv + conv2_bias).astype(jnp.bfloat16)
```

```python
import functools

import jax
import jax.numpy as jnp
from jax.experimental import pallas as pl
from jax.experimental.pallas import tpu as pltpu
from jax import lax
from jax.sharding import PartitionSpec as P

GROUPS = 32
GS = 16


epsilon = 1e-06


def extended(cells, sides, width):
    for axis, dim in sides:
        count = lax.axis_size(axis)
        ends = count - 1
        head = lax.slice_in_dim(cells, 0, width, axis=dim)
        tail = lax.slice_in_dim(cells, cells.shape[dim] - width, cells.shape[dim], axis=dim)
        cells = jnp.concatenate(
            [
                lax.ppermute(tail, axis, [(i, (i + 1) % count) for i in range(ends)]),
                cells,
                lax.ppermute(head, axis, [((i + 1) % count, i) for i in range(ends)]),
            ],
            axis=dim,
        )
    return cells


def unfold(padded, frames, height, breadth):
    pieces = []
    for shift_time in range(3):
        for shift_row in range(3):
            for shift_col in range(3):
                pieces.append(
                    padded[
                        shift_time : shift_time + frames,
                        shift_row : shift_row + height,
                        shift_col : shift_col + breadth,
                        :,
                    ]
                )
    return jnp.concatenate(pieces, axis=-1)


def norm_apply(upsampled, mean_chan, scale_chan, gain, bias):
    scaled = (upsampled.astype(jnp.float32) - mean_chan) * scale_chan
    return jax.nn.silu(scaled * gain + bias).astype(jnp.bfloat16)


def on_device(
    latent,
    cache_mid,
    norm1_gain,
    norm1_bias,
    conv1_weight,
    conv1_bias,
    cache_up,
    norm2_gain,
    norm2_bias,
    conv2_weight,
    conv2_bias,
):
    frames, height, breadth, chan_here = latent.shape
    groups_here = chan_here // GS
    values = latent.astype(jnp.float32)
    grouped = values.reshape(frames, height, breadth, groups_here, GS)
    entries = frames * height * lax.axis_size("space") * breadth * GS
    group_mean = lax.psum(jnp.sum(grouped, axis=(0, 1, 2, 4)), "space") / entries
    centred = grouped - group_mean[:, None]
    group_var = lax.psum(jnp.sum(centred * centred, axis=(0, 1, 2, 4)), "space") / entries
    scaled = (centred * lax.rsqrt(group_var + epsilon)[:, None]).reshape(
        frames, height, breadth, chan_here
    )
    normed_mid = jax.nn.silu(scaled * norm1_gain + norm1_bias).astype(jnp.bfloat16)
    joined = jnp.concatenate([cache_mid, normed_mid], axis=0)
    rimmed = extended(joined, (("space", 1),), 1)
    padded = jnp.pad(rimmed, ((0, 0), (0, 0), (1, 1), (0, 0)))
    columns = unfold(padded, frames, height, breadth).reshape(frames * height * breadth, -1)
    kernel = conv1_weight.reshape(-1, conv1_weight.shape[-1])
    summed = lax.psum_scatter(
        lax.dot_general(
            kernel, columns, (((0,), (1,)), ((), ())), preferred_element_type=jnp.float32
        ),
        "chan",
        scatter_dimension=0,
        tiled=True,
    )
    conv_mid = summed.T.reshape(frames, height, breadth, chan_here)
    merged = (values + conv_mid + conv1_bias).astype(jnp.bfloat16)
    merged_groups = merged.astype(jnp.float32).reshape(frames, height, breadth, groups_here, GS)
    first_group = lax.axis_index("chan") * groups_here

    def place(partial_value):
        return lax.dynamic_update_slice_in_dim(
            jnp.zeros((GROUPS,), jnp.float32), partial_value, first_group, 0
        )

    own_sum = jnp.sum(merged_groups, axis=(0, 1, 2, 4))
    group_sums, group_squares = lax.psum(
        (place(own_sum), place(jnp.sum(merged_groups * merged_groups, axis=(0, 1, 2, 4)))),
        ("space", "chan"),
    )
    up_mean = group_sums / entries
    up_var = group_squares / entries - up_mean * up_mean
    mean_chan = jnp.repeat(up_mean, GS)
    scale_chan = jnp.repeat(lax.rsqrt(up_var + epsilon), GS)
    pixel_tile = lax.all_to_all(merged, "chan", split_axis=2, concat_axis=3, tiled=True)
    upsampled = jnp.repeat(jnp.repeat(pixel_tile, 2, axis=1), 2, axis=2)
    normed_up = norm_apply(upsampled, mean_chan, scale_chan, norm2_gain, norm2_bias)
    joined_up = jnp.concatenate([cache_up, normed_up], axis=0)
    rimmed_up = extended(joined_up, (("space", 1), ("chan", 2)), 1)
    up_height = normed_up.shape[1]
    up_breadth = normed_up.shape[2]
    up_columns = unfold(rimmed_up, frames, up_height, up_breadth).reshape(
        frames * up_height * up_breadth, -1
    )
    kernel_up = conv2_weight.reshape(-1, conv2_weight.shape[-1])
    up_conv = jnp.dot(
        up_columns,
        lax.all_gather(kernel_up, "chan", axis=1, tiled=True),
        preferred_element_type=jnp.float32,
    )
    result = (up_conv + conv2_bias).astype(jnp.bfloat16).reshape(frames, up_height, up_breadth, -1)
    return result


MESH = pl.DeviceIdType.MESH
F32 = jnp.float32
BF16 = jnp.bfloat16


def group_total(row):
    lane = lax.broadcasted_iota(jnp.int32, row.shape, 1)
    width = row.shape[1]
    step = 1
    while step < GS:
        upper = pltpu.roll(row, width - step, 1)
        lower = pltpu.roll(row, step, 1)
        row = row + jnp.where(lane % (2 * step) < step, upper, lower)
        step *= 2
    return row


def local_stats(values):
    count = values.shape[0] * GS
    mean = group_total(jnp.sum(values, axis=0, keepdims=True)) / count
    centred = values - mean
    return mean, group_total(jnp.sum(centred * centred, axis=0, keepdims=True))


def whole_stats(stats_ref, count):
    parts = stats_ref.shape[0]
    means = stats_ref[:, 0:1, :]
    mean = jnp.sum(means, axis=0) / parts
    apart = means - mean[None]
    spread = jnp.sum(stats_ref[:, 1:2, :], axis=0) + count * jnp.sum(apart * apart, axis=0)
    return mean, lax.rsqrt(spread / (count * parts) + epsilon)


def norm_silu(values, mean, scale, gain, bias):
    moved = (values - mean) * scale * gain + bias
    shrunk = jnp.exp(-jnp.abs(moved))
    return (moved * jnp.where(moved < 0, shrunk, 1.0) / (1.0 + shrunk)).astype(BF16)


def from_left(values):
    place = lax.broadcasted_iota(jnp.int32, values.shape, 0)
    return jnp.where(place == 0, 0.0, pltpu.roll(values, 1, 0))


def from_right(values):
    size = values.shape[0]
    place = lax.broadcasted_iota(jnp.int32, values.shape, 0)
    return jnp.where(place == size - 1, 0.0, pltpu.roll(values, size - 1, 0))


def dot(a, b):
    return jnp.dot(a, b, preferred_element_type=F32)


def decoder_kernel(
    rows,
    chans,
    latent,
    cache_mid,
    gain1,
    bias1,
    w1_hbm,
    conv1_bias,
    cache_up,
    gain2,
    bias2,
    w2_hbm,
    conv2_bias,
    out,
    w1,
    w2,
    halo_mid,
    stats1,
    stats2,
    part,
    summands,
    gathered,
    taps,
    rim_out,
    rim_in,
    normed,
    final,
    raised,
    upper_cells,
    lower_cells,
    out_send,
    out_recv,
    load_sem,
    halo_send,
    halo_recv,
    stat_send,
    stat_recv,
    sum_send,
    sum_recv,
    cache_send,
    cache_recv,
    rim_send,
    rim_recv,
    norm_send,
    norm_recv,
    last_send,
    last_recv,
):
    breadth, chan_here = latent.shape
    r = lax.axis_index("space")
    c = lax.axis_index("chan")
    has = (r > 0, r < rows - 1)
    beside = (r - 1, r + 1)
    mate = c + 1 - 2 * (c % 2)
    across = (c + 2) % chans

    def remote(src, dst, send, recv, **where):
        return pltpu.make_async_remote_copy(
            src_ref=src,
            dst_ref=dst,
            send_sem=send,
            recv_sem=recv,
            device_id=where,
            device_id_type=MESH,
        )

    load1 = pltpu.make_async_copy(w1_hbm, w1, load_sem.at[0])
    load2 = pltpu.make_async_copy(w2_hbm, w2, load_sem.at[1])
    load1.start()
    load2.start()

    barrier = pltpu.get_barrier_semaphore()
    for k in range(1, rows):
        pl.semaphore_signal(
            barrier, inc=1, device_id={"space": (r + k) % rows}, device_id_type=MESH
        )
    for k in range(1, chans):
        pl.semaphore_signal(
            barrier, inc=1, device_id={"chan": (c + k) % chans}, device_id_type=MESH
        )
    for side in range(2):

        @pl.when(has[side])
        def _():
            for k in range(1, chans):
                pl.semaphore_signal(
                    barrier,
                    inc=1,
                    device_id={"space": beside[side], "chan": (c + k) % chans},
                    device_id_type=MESH,
                )

    values = latent[...].astype(F32)
    mean, spread = local_stats(values)
    stats1[0, 0:1, :] = mean
    stats1[0, 1:2, :] = spread
    taps[...] = jnp.zeros_like(taps)
    for side in range(2):

        @pl.when(jnp.logical_not(has[side]))
        def _():
            halo_mid[side] = jnp.zeros(halo_mid.shape[1:], BF16)
            rim_in[side] = jnp.zeros(rim_in.shape[1:], F32)
            normed[2 * side] = jnp.zeros(normed.shape[1:], BF16)

    sides = has[0].astype(jnp.int32) + has[1].astype(jnp.int32)
    pl.semaphore_wait(barrier, rows - 1 + (chans - 1) * (1 + sides))

    def share(stats, which):
        copies = []
        for k in range(1, rows):
            copy = remote(
                stats.at[0],
                stats.at[k],
                stat_send.at[which, k],
                stat_recv.at[which, k],
                space=(r + k) % rows,
            )
            copy.start()
            copies.append(copy)
        return copies

    first_stats = share(stats1, 0)

    def halo_copies(side):
        return (
            remote(
                cache_mid,
                halo_mid.at[1 - side, pl.ds(0, 2)],
                halo_send.at[side, 0],
                halo_recv.at[1 - side, 0],
                space=beside[side],
            ),
            remote(
                latent,
                halo_mid.at[1 - side, 2],
                halo_send.at[side, 1],
                halo_recv.at[1 - side, 1],
                space=beside[side],
            ),
        )

    def halo_arrivals(side):
        return (
            remote(
                cache_mid,
                halo_mid.at[side, pl.ds(0, 2)],
                halo_send.at[side, 0],
                halo_recv.at[side, 0],
                space=beside[side],
            ),
            remote(
                latent,
                halo_mid.at[side, 2],
                halo_send.at[side, 1],
                halo_recv.at[side, 1],
                space=beside[side],
            ),
        )

    for side in range(2):

        @pl.when(has[side])
        def _():
            for copy in halo_copies(side):
                copy.start()

    own_across = remote(
        cache_up, gathered.at[c], cache_send.at[0], cache_recv.at[0], chan=across
    )
    own_mate = remote(cache_up, gathered.at[c], cache_send.at[1], cache_recv.at[1], chan=mate)
    passed = remote(
        gathered.at[across], gathered.at[across], cache_send.at[2], cache_recv.at[2], chan=mate
    )
    own_across.start()
    own_mate.start()
    gathered[c] = cache_up[...]

    for side in range(2):

        @pl.when(has[side])
        def _():
            for copy in halo_arrivals(side):
                copy.wait_recv()

    def mid_taps(pieces, frames):
        cells = jnp.concatenate(pieces, axis=1)
        products = []
        for dx in range(3):
            weights = w1[frames, :, dx].reshape(cells.shape[1], w1.shape[-1])
            products.append(dot(cells, weights))
        return from_left(products[0]) + products[1] + from_right(products[2])

    load1.wait()
    pieces = []
    for frame in range(2):
        pieces += [halo_mid[0, frame], cache_mid[frame], halo_mid[1, frame]]
    cached_mid = mid_taps(pieces, slice(0, 2))

    for copy in first_stats:
        copy.wait_recv()
    mean, scale = whole_stats(stats1, breadth * GS)
    pieces = []
    for side in range(2):
        rim = norm_silu(halo_mid[side, 2].astype(F32), mean, scale, gain1[...], bias1[...])
        pieces.append(jnp.where(has[side], rim.astype(F32), 0.0).astype(BF16))
    pieces.insert(1, norm_silu(values, mean, scale, gain1[...], bias1[...]))
    partial = cached_mid + mid_taps(pieces, slice(2, 3))
    for block in range(chans):
        part[block] = partial[:, block * chan_here : (block + 1) * chan_here]
    sums = []
    for k in (2, 3, 1):
        to = (c + k) % chans
        copy = remote(part.at[to], summands.at[c], sum_send.at[k], sum_recv.at[k], chan=to)
        copy.start()
        sums.append(copy)
    summands[c] = part[c]

    def up_taps(base):
        def step(index, _):
            frame = index // 3
            dy = index % 3
            cells = gathered[pl.ds(base, 2), frame]
            cells = cells.reshape(-1, cells.shape[-1])
            weights = jnp.concatenate([w2[frame, dy, dx] for dx in range(3)], axis=1)
            product = dot(cells, weights).reshape((2, 2) + taps.shape[2:])
            for row in range(2):
                taps[row + 2 - dy, pl.ds(base, 2)] += product[:, row]
            return 0

        lax.fori_loop(0, 6, step, 0)

    base = c - c % 2
    load2.wait()
    own_mate.wait_recv()
    up_taps(base)
    own_across.wait_recv()
    passed.start()

    for copy in sums:
        copy.wait_recv()
    conv_mid = summands[0]
    for block in range(1, chans):
        conv_mid = conv_mid + summands[block]
    merged = (values + conv_mid + conv1_bias[...]).astype(BF16).astype(F32)
    mean, spread = local_stats(merged)
    stats2[0, 0:1, :] = mean
    stats2[0, 1:2, :] = spread
    second_stats = share(stats2, 1)

    passed.wait_recv()
    up_taps((base + 2) % chans)

    def combined(row):
        cells = taps[row].reshape(-1, taps.shape[-1])
        lanes = [cells[:, dx * chan_here : (dx + 1) * chan_here] for dx in range(3)]
        return from_left(lanes[0]) + lanes[1] + from_right(lanes[2])

    for side in range(2):
        rim_out[side] = combined(3 * side)
        final[side] = combined(1 + side) + conv2_bias[c]

    for copy in second_stats:
        copy.wait_recv()
    mean, scale = whole_stats(stats2, breadth * GS)
    normed[1, c] = norm_silu(merged, mean, scale, gain2[c], bias2[c])

    def spread_normed(row, k, **where):
        return remote(
            normed.at[1, c], normed.at[row, c], norm_send.at[row, k], norm_recv.at[row, k], **where
        )

    def rim_copy(side):
        return remote(
            rim_out.at[side],
            rim_in.at[1 - side],
            rim_send.at[side],
            rim_recv.at[1 - side],
            space=beside[side],
        )

    def rim_arrival(side):
        return remote(
            rim_out.at[side],
            rim_in.at[side],
            rim_send.at[side],
            rim_recv.at[side],
            space=beside[side],
        )

    along = []
    for k in (2, 3, 1):
        copy = spread_normed(1, k, chan=(c + k) % chans)
        copy.start()
        along.append(copy)

    def to_side(side, k):
        return spread_normed(
            2 * (1 - side), k, space=beside[side], chan=(c + k) % chans
        )

    for k in (2, 3, 1, 0):
        for side in range(2):

            @pl.when(has[side])
            def _():
                to_side(side, k).start()

    for side in range(2):

        @pl.when(has[side])
        def _():
            rim_copy(side).start()

    def raise_taps(row, dy, slot):
        cells = jnp.concatenate([normed[row, block] for block in range(chans)], axis=1)
        weights = jnp.concatenate([w2[2, dy, dx] for dx in range(3)], axis=1)
        raised[slot] = dot(cells, weights)

    def raise_centre(dy, _):
        raise_taps(1, dy, dy)
        return 0

    def raise_rim(side, _):
        raise_taps(2 * side, 2 * side, 3 + side)
        return 0

    for copy in along:
        copy.wait_recv()
    lax.fori_loop(0, 3, raise_centre, 0)

    for side in range(2):

        @pl.when(has[side])
        def _():
            for k in range(chans):
                spread_normed(2 * side, k, space=beside[side], chan=c).wait_recv()

    lax.fori_loop(0, 2, raise_rim, 0)

    for side in range(2):

        @pl.when(has[side])
        def _():
            rim_arrival(side).wait_recv()

    for row in range(2):
        product = raised[1] + raised[2 * (1 - row)] + raised[3 + row]
        lanes = [product[:, dx * chan_here : (dx + 1) * chan_here] for dx in range(3)]
        even = from_left(lanes[0]) + lanes[1] + lanes[2]
        odd = lanes[0] + lanes[1] + from_right(lanes[2])
        woven = (upper_cells, lower_cells)[row]
        woven[pl.ds(0, breadth, stride=2), :] = even
        woven[pl.ds(1, breadth, stride=2), :] = odd
        result = (final[row] + rim_in[row] + woven[...]).astype(BF16)
        share_cols = out.shape[1]
        for block in range(chans):
            out_send[block, row] = result[block * share_cols : (block + 1) * share_cols]

    lasts = []
    for k in (2, 3, 1):
        to = (c + k) % chans
        copy = remote(out_send.at[to], out_recv.at[c], last_send.at[k], last_recv.at[k], chan=to)
        copy.start()
        lasts.append(copy)
    out_recv[c] = out_send[c]

    for copy in first_stats + second_stats + sums + along + [own_across, own_mate, passed]:
        copy.wait_send()
    for side in range(2):

        @pl.when(has[side])
        def _():
            for copy in halo_copies(side):
                copy.wait_send()
            for k in range(chans):
                to_side(side, k).wait_send()
            rim_copy(side).wait_send()

    for copy in lasts:
        copy.wait_recv()
    for block in range(chans):
        out[:, :, block * chan_here : (block + 1) * chan_here] = out_recv[block]
    for copy in lasts:
        copy.wait_send()


def fused_on_device(
    rows,
    chans,
    latent,
    cache_mid,
    norm1_gain,
    norm1_bias,
    conv1_weight,
    conv1_bias,
    cache_up,
    norm2_gain,
    norm2_bias,
    conv2_weight,
    conv2_bias,
):
    breadth, chan_here = latent.shape[2:]
    up_rows, up_cols, chan_all = cache_up.shape[1:]
    vmem = pl.BlockSpec(memory_space=pltpu.VMEM)
    hbm = pl.BlockSpec(memory_space=pl.ANY)
    dma = pltpu.SemaphoreType.DMA
    result = pl.pallas_call(
        functools.partial(decoder_kernel, rows, chans),
        out_shape=jax.ShapeDtypeStruct((up_rows, up_cols, chan_all), BF16),
        in_specs=[vmem, vmem, vmem, vmem, hbm, vmem, vmem, vmem, vmem, hbm, vmem],
        out_specs=vmem,
        scratch_shapes=[
            pltpu.VMEM(conv1_weight.shape, BF16),
            pltpu.VMEM(conv2_weight.shape, BF16),
            pltpu.VMEM((2, 3, breadth, chan_here), BF16),
            pltpu.VMEM((rows, 8, chan_here), F32),
            pltpu.VMEM((rows, 8, chan_here), F32),
            pltpu.VMEM((chans, breadth, chan_here), F32),
            pltpu.VMEM((chans, breadth, chan_here), F32),
            pltpu.VMEM((chans,) + cache_up.shape, BF16),
            pltpu.VMEM((4, chans, up_cols, 3 * chan_here), F32),
            pltpu.VMEM((2, 2 * breadth, chan_here), F32),
            pltpu.VMEM((2, 2 * breadth, chan_here), F32),
            pltpu.VMEM((3, chans, breadth, chan_here), BF16),
            pltpu.VMEM((2, 2 * breadth, chan_here), F32),
            pltpu.VMEM((5, breadth, 3 * chan_here), F32),
            pltpu.VMEM((2 * breadth, chan_here), F32),
            pltpu.VMEM((2 * breadth, chan_here), F32),
            pltpu.VMEM((chans, up_rows, up_cols, chan_here), BF16),
            pltpu.VMEM((chans, up_rows, up_cols, chan_here), BF16),
            dma((2,)),
            dma((2, 2)),
            dma((2, 2)),
            dma((2, rows)),
            dma((2, rows)),
            dma((chans,)),
            dma((chans,)),
            dma((3,)),
            dma((3,)),
            dma((2,)),
            dma((2,)),
            dma((3, chans)),
            dma((3, chans)),
            dma((chans,)),
            dma((chans,)),
        ],
        compiler_params=pltpu.CompilerParams(
            collective_id=0, has_side_effects=True, vmem_limit_bytes=48 * 2**20
        ),
    )(
        latent[0, 0],
        cache_mid[:, 0],
        norm1_gain[None],
        norm1_bias[None],
        conv1_weight,
        conv1_bias[None],
        cache_up,
        norm2_gain.reshape(chans, 1, chan_here),
        norm2_bias.reshape(chans, 1, chan_here),
        conv2_weight,
        conv2_bias.reshape(chans, 1, chan_here),
    )
    return result[None]


def fits_kernel(
    rows, chans, latent, cache_up
):
    return (
        latent.shape[:2] == (1, 1)
        and cache_up.shape[:2] == (2, 2)
        and chans == 4
        and rows > 1
        and latent.shape[3] == 128
        and cache_up.shape[2] % 16 == 0
    )


def solution(mesh):
    placed = (
        P(None, "space", None, "chan"),
        P(None, "space", None, "chan"),
        P("chan"),
        P("chan"),
        P(None, None, None, "chan", None),
        P("chan"),
        P(None, "space", "chan", None),
        P(),
        P(),
        P(None, None, None, None, "chan"),
        P(),
    )
    rows = mesh.shape["space"]
    chans = mesh.shape["chan"]

    def one_device(*args):
        if fits_kernel(rows, chans, args[0], args[6]):
            return fused_on_device(rows, chans, *args)
        return on_device(*args)

    return jax.shard_map(
        one_device,
        mesh=mesh,
        in_specs=placed,
        out_specs=P(None, "space", "chan", None),
        check_vma=False,
    )
```

```python
import functools

import jax
import jax.numpy as jnp
from jax.experimental import pallas as pl
from jax.experimental.pallas import tpu as pltpu
from jax import lax
from jax.sharding import PartitionSpec as P

GROUPS = 32
GS = 16


epsilon = 1e-06


def extended(cells, sides, width):
    for axis, dim in sides:
        count = lax.axis_size(axis)
        ends = count - 1
        head = lax.slice_in_dim(cells, 0, width, axis=dim)
        tail = lax.slice_in_dim(cells, cells.shape[dim] - width, cells.shape[dim], axis=dim)
        cells = jnp.concatenate(
            [
                lax.ppermute(tail, axis, [(i, (i + 1) % count) for i in range(ends)]),
                cells,
                lax.ppermute(head, axis, [((i + 1) % count, i) for i in range(ends)]),
            ],
            axis=dim,
        )
    return cells


def unfold(padded, frames, height, breadth):
    pieces = []
    for shift_time in range(3):
        for shift_row in range(3):
            for shift_col in range(3):
                pieces.append(
                    padded[
                        shift_time : shift_time + frames,
                        shift_row : shift_row + height,
                        shift_col : shift_col + breadth,
                        :,
                    ]
                )
    return jnp.concatenate(pieces, axis=-1)


def norm_apply(upsampled, mean_chan, scale_chan, gain, bias):
    scaled = (upsampled.astype(jnp.float32) - mean_chan) * scale_chan
    return jax.nn.silu(scaled * gain + bias).astype(jnp.bfloat16)


def on_device(
    latent,
    cache_mid,
    norm1_gain,
    norm1_bias,
    conv1_weight,
    conv1_bias,
    cache_up,
    norm2_gain,
    norm2_bias,
    conv2_weight,
    conv2_bias,
):
    frames, height, breadth, chan_here = latent.shape
    groups_here = chan_here // GS
    values = latent.astype(jnp.float32)
    grouped = values.reshape(frames, height, breadth, groups_here, GS)
    entries = frames * height * lax.axis_size("space") * breadth * GS
    group_mean = lax.psum(jnp.sum(grouped, axis=(0, 1, 2, 4)), "space") / entries
    centred = grouped - group_mean[:, None]
    group_var = lax.psum(jnp.sum(centred * centred, axis=(0, 1, 2, 4)), "space") / entries
    scaled = (centred * lax.rsqrt(group_var + epsilon)[:, None]).reshape(
        frames, height, breadth, chan_here
    )
    normed_mid = jax.nn.silu(scaled * norm1_gain + norm1_bias).astype(jnp.bfloat16)
    joined = jnp.concatenate([cache_mid, normed_mid], axis=0)
    rimmed = extended(joined, (("space", 1),), 1)
    padded = jnp.pad(rimmed, ((0, 0), (0, 0), (1, 1), (0, 0)))
    columns = unfold(padded, frames, height, breadth).reshape(frames * height * breadth, -1)
    kernel = conv1_weight.reshape(-1, conv1_weight.shape[-1])
    summed = lax.psum_scatter(
        lax.dot_general(
            kernel, columns, (((0,), (1,)), ((), ())), preferred_element_type=jnp.float32
        ),
        "chan",
        scatter_dimension=0,
        tiled=True,
    )
    conv_mid = summed.T.reshape(frames, height, breadth, chan_here)
    merged = (values + conv_mid + conv1_bias).astype(jnp.bfloat16)
    merged_groups = merged.astype(jnp.float32).reshape(frames, height, breadth, groups_here, GS)
    first_group = lax.axis_index("chan") * groups_here

    def place(partial_value):
        return lax.dynamic_update_slice_in_dim(
            jnp.zeros((GROUPS,), jnp.float32), partial_value, first_group, 0
        )

    own_sum = jnp.sum(merged_groups, axis=(0, 1, 2, 4))
    group_sums, group_squares = lax.psum(
        (place(own_sum), place(jnp.sum(merged_groups * merged_groups, axis=(0, 1, 2, 4)))),
        ("space", "chan"),
    )
    up_mean = group_sums / entries
    up_var = group_squares / entries - up_mean * up_mean
    mean_chan = jnp.repeat(up_mean, GS)
    scale_chan = jnp.repeat(lax.rsqrt(up_var + epsilon), GS)
    pixel_tile = lax.all_to_all(merged, "chan", split_axis=2, concat_axis=3, tiled=True)
    upsampled = jnp.repeat(jnp.repeat(pixel_tile, 2, axis=1), 2, axis=2)
    normed_up = norm_apply(upsampled, mean_chan, scale_chan, norm2_gain, norm2_bias)
    joined_up = jnp.concatenate([cache_up, normed_up], axis=0)
    rimmed_up = extended(joined_up, (("space", 1), ("chan", 2)), 1)
    up_height = normed_up.shape[1]
    up_breadth = normed_up.shape[2]
    up_columns = unfold(rimmed_up, frames, up_height, up_breadth).reshape(
        frames * up_height * up_breadth, -1
    )
    kernel_up = conv2_weight.reshape(-1, conv2_weight.shape[-1])
    up_conv = jnp.dot(
        up_columns,
        lax.all_gather(kernel_up, "chan", axis=1, tiled=True),
        preferred_element_type=jnp.float32,
    )
    result = (up_conv + conv2_bias).astype(jnp.bfloat16).reshape(frames, up_height, up_breadth, -1)
    return result


MESH = pl.DeviceIdType.MESH
F32 = jnp.float32
BF16 = jnp.bfloat16


def group_total(row):
    lane = lax.broadcasted_iota(jnp.int32, row.shape, 1)
    width = row.shape[1]
    step = 1
    while step < GS:
        upper = pltpu.roll(row, width - step, 1)
        lower = pltpu.roll(row, step, 1)
        row = row + jnp.where(lane % (2 * step) < step, upper, lower)
        step *= 2
    return row


def local_stats(values):
    count = values.shape[0] * GS
    mean = group_total(jnp.sum(values, axis=0, keepdims=True)) / count
    centred = values - mean
    return mean, group_total(jnp.sum(centred * centred, axis=0, keepdims=True))


def whole_stats(stats_ref, count):
    parts = stats_ref.shape[0]
    means = stats_ref[:, 0:1, :]
    mean = jnp.sum(means, axis=0) / parts
    apart = means - mean[None]
    spread = jnp.sum(stats_ref[:, 1:2, :], axis=0) + count * jnp.sum(apart * apart, axis=0)
    return mean, lax.rsqrt(spread / (count * parts) + epsilon)


def norm_silu(values, mean, scale, gain, bias):
    moved = (values - mean) * scale * gain + bias
    shrunk = jnp.exp(-jnp.abs(moved))
    return (moved * jnp.where(moved < 0, shrunk, 1.0) / (1.0 + shrunk)).astype(BF16)


def from_left(values):
    place = lax.broadcasted_iota(jnp.int32, values.shape, 0)
    return jnp.where(place == 0, 0.0, pltpu.roll(values, 1, 0))


def from_right(values):
    size = values.shape[0]
    place = lax.broadcasted_iota(jnp.int32, values.shape, 0)
    return jnp.where(place == size - 1, 0.0, pltpu.roll(values, size - 1, 0))


def dot(a, b):
    return jnp.dot(a, b, preferred_element_type=F32)


def decoder_kernel(
    rows,
    chans,
    latent_hbm,
    cache_mid_hbm,
    gain1_hbm,
    bias1_hbm,
    w1_hbm,
    conv1_bias_hbm,
    cache_up,
    gain2_hbm,
    bias2_hbm,
    w2_hbm,
    conv2_bias_hbm,
    out,
    latent,
    cache_mid,
    gain1,
    bias1,
    conv1_bias,
    gain2,
    bias2,
    conv2_bias,
    w1,
    w2,
    halo_mid,
    stats1,
    stats2,
    part,
    summands,
    gathered,
    taps,
    rim_out,
    rim_in,
    normed,
    final,
    raised,
    upper_cells,
    lower_cells,
    above_cells,
    below_cells,
    out_send,
    out_recv,
    load_sem,
    halo_send,
    halo_recv,
    stat_send,
    stat_recv,
    sum_send,
    sum_recv,
    cache_send,
    cache_recv,
    rim_send,
    rim_recv,
    norm_send,
    norm_recv,
    last_send,
    last_recv,
):
    breadth, chan_here = latent.shape
    r = lax.axis_index("space")
    c = lax.axis_index("chan")
    has = (r > 0, r < rows - 1)
    beside = (r - 1, r + 1)
    mate = c + 1 - 2 * (c % 2)
    across = (c + 2) % chans

    def remote(src, dst, send, recv, **where):
        return pltpu.make_async_remote_copy(
            src_ref=src,
            dst_ref=dst,
            send_sem=send,
            recv_sem=recv,
            device_id=where,
            device_id_type=MESH,
        )

    moves = (
        (latent_hbm, latent),
        (w1_hbm, w1),
        (cache_mid_hbm, cache_mid),
        (gain1_hbm, gain1),
        (bias1_hbm, bias1),
        (conv1_bias_hbm, conv1_bias),
        (gain2_hbm, gain2),
        (bias2_hbm, bias2),
        (conv2_bias_hbm, conv2_bias),
        (cache_up, gathered.at[c]),
        (w2_hbm, w2),
    )
    loads = [
        pltpu.make_async_copy(source, target, load_sem.at[index])
        for index, (source, target) in enumerate(moves)
    ]
    for load in loads:
        load.start()

    barrier = pltpu.get_barrier_semaphore()
    for k in range(1, rows):
        pl.semaphore_signal(
            barrier, inc=1, device_id={"space": (r + k) % rows}, device_id_type=MESH
        )
    for k in range(1, chans):
        pl.semaphore_signal(
            barrier, inc=1, device_id={"chan": (c + k) % chans}, device_id_type=MESH
        )
    loads[0].wait()
    values = latent[...].astype(F32)
    mean, spread = local_stats(values)
    stats1[0, 0:1, :] = mean
    stats1[0, 1:2, :] = spread
    taps[...] = jnp.zeros_like(taps)
    for side in range(2):

        @pl.when(jnp.logical_not(has[side]))
        def _():
            halo_mid[side] = jnp.zeros(halo_mid.shape[1:], BF16)
            rim_in[side] = jnp.zeros(rim_in.shape[1:], F32)

    pl.semaphore_wait(barrier, rows - 1 + chans - 1)

    def share(stats, which):
        copies = []
        for k in range(1, rows):
            copy = remote(
                stats.at[0],
                stats.at[k],
                stat_send.at[which, k],
                stat_recv.at[which, k],
                space=(r + k) % rows,
            )
            copy.start()
            copies.append(copy)
        return copies

    first_stats = share(stats1, 0)

    def halo_copies(side):
        return (
            remote(
                cache_mid_hbm,
                halo_mid.at[1 - side, pl.ds(0, 2)],
                halo_send.at[side, 0],
                halo_recv.at[1 - side, 0],
                space=beside[side],
            ),
            remote(
                latent_hbm,
                halo_mid.at[1 - side, 2],
                halo_send.at[side, 1],
                halo_recv.at[1 - side, 1],
                space=beside[side],
            ),
        )

    def halo_arrivals(side):
        return (
            remote(
                cache_mid_hbm,
                halo_mid.at[side, pl.ds(0, 2)],
                halo_send.at[side, 0],
                halo_recv.at[side, 0],
                space=beside[side],
            ),
            remote(
                latent_hbm,
                halo_mid.at[side, 2],
                halo_send.at[side, 1],
                halo_recv.at[side, 1],
                space=beside[side],
            ),
        )

    for side in range(2):

        @pl.when(has[side])
        def _():
            for copy in halo_copies(side):
                copy.start()

    own_across = remote(
        cache_up, gathered.at[c], cache_send.at[0], cache_recv.at[0], chan=across
    )
    own_mate = remote(cache_up, gathered.at[c], cache_send.at[1], cache_recv.at[1], chan=mate)
    passed = remote(
        gathered.at[across], gathered.at[across], cache_send.at[2], cache_recv.at[2], chan=mate
    )
    own_across.start()
    own_mate.start()
    for load in loads[1:-1]:
        load.wait()

    for side in range(2):

        @pl.when(has[side])
        def _():
            for copy in halo_arrivals(side):
                copy.wait_recv()

    def mid_taps(pieces, frames):
        cells = jnp.concatenate(pieces, axis=1)
        products = []
        for dx in range(3):
            weights = w1[frames, :, dx].reshape(cells.shape[1], w1.shape[-1])
            products.append(dot(cells, weights))
        return from_left(products[0]) + products[1] + from_right(products[2])

    pieces = []
    for frame in range(2):
        pieces += [halo_mid[0, frame], cache_mid[frame], halo_mid[1, frame]]
    cached_mid = mid_taps(pieces, slice(0, 2))

    for copy in first_stats:
        copy.wait_recv()
    mean, scale = whole_stats(stats1, breadth * GS)
    pieces = []
    for side in range(2):
        rim = norm_silu(halo_mid[side, 2].astype(F32), mean, scale, gain1[...], bias1[...])
        pieces.append(jnp.where(has[side], rim.astype(F32), 0.0).astype(BF16))
    pieces.insert(1, norm_silu(values, mean, scale, gain1[...], bias1[...]))
    partial = cached_mid + mid_taps(pieces, slice(2, 3))
    for block in range(chans):
        part[block] = partial[:, block * chan_here : (block + 1) * chan_here]
    sums = []
    for k in (2, 3, 1):
        to = (c + k) % chans
        copy = remote(part.at[to], summands.at[c], sum_send.at[k], sum_recv.at[k], chan=to)
        copy.start()
        sums.append(copy)
    summands[c] = part[c]

    def up_taps(base):
        def step(index, _):
            frame = index // 3
            dy = index % 3
            cells = gathered[pl.ds(base, 2), frame]
            cells = cells.reshape(-1, cells.shape[-1])
            weights = jnp.concatenate([w2[frame, dy, dx] for dx in range(3)], axis=1)
            product = dot(cells, weights).reshape((2, 2) + taps.shape[2:])
            for row in range(2):
                taps[row + 2 - dy, pl.ds(base, 2)] += product[:, row]
            return 0

        lax.fori_loop(0, 6, step, 0)

    base = c - c % 2
    loads[-1].wait()
    own_mate.wait_recv()
    up_taps(base)
    own_across.wait_recv()
    passed.start()

    for copy in sums:
        copy.wait_recv()
    conv_mid = summands[0]
    for block in range(1, chans):
        conv_mid = conv_mid + summands[block]
    merged = (values + conv_mid + conv1_bias[...]).astype(BF16).astype(F32)
    mean, spread = local_stats(merged)
    stats2[0, 0:1, :] = mean
    stats2[0, 1:2, :] = spread
    second_stats = share(stats2, 1)

    passed.wait_recv()
    up_taps((base + 2) % chans)

    def combined(row):
        cells = taps[row].reshape(-1, taps.shape[-1])
        lanes = [cells[:, dx * chan_here : (dx + 1) * chan_here] for dx in range(3)]
        return from_left(lanes[0]) + lanes[1] + from_right(lanes[2])

    for side in range(2):
        rim_out[side] = combined(3 * side)
        final[side] = combined(1 + side) + conv2_bias[c]

    for copy in second_stats:
        copy.wait_recv()
    mean, scale = whole_stats(stats2, breadth * GS)
    normed[c] = norm_silu(merged, mean, scale, gain2[c], bias2[c])

    def rim_copy(side):
        return remote(
            rim_out.at[side],
            rim_in.at[1 - side],
            rim_send.at[side],
            rim_recv.at[1 - side],
            space=beside[side],
        )

    def rim_arrival(side):
        return remote(
            rim_out.at[side],
            rim_in.at[side],
            rim_send.at[side],
            rim_recv.at[side],
            space=beside[side],
        )

    along = []
    for k in (2, 3, 1):
        copy = remote(
            normed.at[c], normed.at[c], norm_send.at[k], norm_recv.at[k], chan=(c + k) % chans
        )
        copy.start()
        along.append(copy)

    def raise_taps(dy, _):
        cells = jnp.concatenate([normed[block] for block in range(chans)], axis=1)
        weights = jnp.concatenate([w2[2, dy, dx] for dx in range(3)], axis=1)
        raised[dy] = dot(cells, weights)
        return 0

    def weave(product, woven):
        lanes = [product[:, dx * chan_here : (dx + 1) * chan_here] for dx in range(3)]
        woven[pl.ds(0, breadth, stride=2), :] = from_left(lanes[0]) + lanes[1] + lanes[2]
        woven[pl.ds(1, breadth, stride=2), :] = lanes[0] + lanes[1] + from_right(lanes[2])

    for copy in along:
        copy.wait_recv()
    lax.fori_loop(0, 3, raise_taps, 0)
    for side, woven in enumerate((above_cells, below_cells)):
        weave(raised[2 * (1 - side)], woven)
        rim_out[side] += woven[...]

        @pl.when(has[side])
        def _():
            rim_copy(side).start()

    for row, woven in enumerate((upper_cells, lower_cells)):
        weave(raised[1] + raised[2 * (1 - row)], woven)
        final[row] += woven[...]

    for side in range(2):

        @pl.when(has[side])
        def _():
            rim_arrival(side).wait_recv()

    for row in range(2):
        result = (final[row] + rim_in[row]).astype(BF16)
        share_cols = out.shape[1]
        for block in range(chans):
            out_send[block, row] = result[block * share_cols : (block + 1) * share_cols]

    lasts = []
    for k in (2, 3, 1):
        to = (c + k) % chans
        copy = remote(out_send.at[to], out_recv.at[c], last_send.at[k], last_recv.at[k], chan=to)
        copy.start()
        lasts.append(copy)
    out_recv[c] = out_send[c]

    for copy in first_stats + second_stats + sums + along + [own_across, own_mate, passed]:
        copy.wait_send()
    for side in range(2):

        @pl.when(has[side])
        def _():
            for copy in halo_copies(side):
                copy.wait_send()
            rim_copy(side).wait_send()

    for copy in lasts:
        copy.wait_recv()
    for block in range(chans):
        out[:, :, block * chan_here : (block + 1) * chan_here] = out_recv[block]
    for copy in lasts:
        copy.wait_send()


def fused_on_device(
    rows,
    chans,
    latent,
    cache_mid,
    norm1_gain,
    norm1_bias,
    conv1_weight,
    conv1_bias,
    cache_up,
    norm2_gain,
    norm2_bias,
    conv2_weight,
    conv2_bias,
):
    breadth, chan_here = latent.shape[2:]
    up_rows, up_cols, chan_all = cache_up.shape[1:]
    vmem = pl.BlockSpec(memory_space=pltpu.VMEM)
    hbm = pl.BlockSpec(memory_space=pltpu.HBM)
    dma = pltpu.SemaphoreType.DMA
    result = pl.pallas_call(
        functools.partial(decoder_kernel, rows, chans),
        out_shape=jax.ShapeDtypeStruct((up_rows, up_cols, chan_all), BF16),
        in_specs=[hbm] * 11,
        out_specs=vmem,
        scratch_shapes=[
            pltpu.VMEM((breadth, chan_here), BF16),
            pltpu.VMEM((2, breadth, chan_here), BF16),
            pltpu.VMEM((1, chan_here), F32),
            pltpu.VMEM((1, chan_here), F32),
            pltpu.VMEM((1, chan_here), F32),
            pltpu.VMEM((chans, 1, chan_here), F32),
            pltpu.VMEM((chans, 1, chan_here), F32),
            pltpu.VMEM((chans, 1, chan_here), F32),
            pltpu.VMEM(conv1_weight.shape, BF16),
            pltpu.VMEM(conv2_weight.shape, BF16),
            pltpu.VMEM((2, 3, breadth, chan_here), BF16),
            pltpu.VMEM((rows, 8, chan_here), F32),
            pltpu.VMEM((rows, 8, chan_here), F32),
            pltpu.VMEM((chans, breadth, chan_here), F32),
            pltpu.VMEM((chans, breadth, chan_here), F32),
            pltpu.VMEM((chans,) + cache_up.shape, BF16),
            pltpu.VMEM((4, chans, up_cols, 3 * chan_here), F32),
            pltpu.VMEM((2, 2 * breadth, chan_here), F32),
            pltpu.VMEM((2, 2 * breadth, chan_here), F32),
            pltpu.VMEM((chans, breadth, chan_here), BF16),
            pltpu.VMEM((2, 2 * breadth, chan_here), F32),
            pltpu.VMEM((3, breadth, 3 * chan_here), F32),
            pltpu.VMEM((2 * breadth, chan_here), F32),
            pltpu.VMEM((2 * breadth, chan_here), F32),
            pltpu.VMEM((2 * breadth, chan_here), F32),
            pltpu.VMEM((2 * breadth, chan_here), F32),
            pltpu.VMEM((chans, up_rows, up_cols, chan_here), BF16),
            pltpu.VMEM((chans, up_rows, up_cols, chan_here), BF16),
            dma((11,)),
            dma((2, 2)),
            dma((2, 2)),
            dma((2, rows)),
            dma((2, rows)),
            dma((chans,)),
            dma((chans,)),
            dma((3,)),
            dma((3,)),
            dma((2,)),
            dma((2,)),
            dma((chans,)),
            dma((chans,)),
            dma((chans,)),
            dma((chans,)),
        ],
        compiler_params=pltpu.CompilerParams(
            collective_id=0, has_side_effects=True, vmem_limit_bytes=56 * 2**20
        ),
    )(
        latent[0, 0],
        cache_mid[:, 0],
        norm1_gain[None],
        norm1_bias[None],
        conv1_weight,
        conv1_bias[None],
        cache_up,
        norm2_gain.reshape(chans, 1, chan_here),
        norm2_bias.reshape(chans, 1, chan_here),
        conv2_weight,
        conv2_bias.reshape(chans, 1, chan_here),
    )
    return result[None]


def fits_kernel(
    rows, chans, latent, cache_up
):
    return (
        latent.shape[:2] == (1, 1)
        and cache_up.shape[:2] == (2, 2)
        and chans == 4
        and rows > 1
        and latent.shape[3] == 128
        and cache_up.shape[2] % 16 == 0
    )


def solution(mesh):
    placed = (
        P(None, "space", None, "chan"),
        P(None, "space", None, "chan"),
        P("chan"),
        P("chan"),
        P(None, None, None, "chan", None),
        P("chan"),
        P(None, "space", "chan", None),
        P(),
        P(),
        P(None, None, None, None, "chan"),
        P(),
    )
    rows = mesh.shape["space"]
    chans = mesh.shape["chan"]

    def one_device(*args):
        if fits_kernel(rows, chans, args[0], args[6]):
            return fused_on_device(rows, chans, *args)
        return on_device(*args)

    return jax.shard_map(
        one_device,
        mesh=mesh,
        in_specs=placed,
        out_specs=P(None, "space", "chan", None),
        check_vma=False,
    )
```

```python
import functools

import jax
import jax.numpy as jnp
from jax.experimental import pallas as pl
from jax.experimental.pallas import tpu as pltpu
from jax import lax
from jax.sharding import PartitionSpec as P

GROUPS = 32
GS = 16


epsilon = 1e-06


def extended(cells, sides, width):
    for axis, dim in sides:
        count = lax.axis_size(axis)
        ends = count - 1
        head = lax.slice_in_dim(cells, 0, width, axis=dim)
        tail = lax.slice_in_dim(cells, cells.shape[dim] - width, cells.shape[dim], axis=dim)
        cells = jnp.concatenate(
            [
                lax.ppermute(tail, axis, [(i, (i + 1) % count) for i in range(ends)]),
                cells,
                lax.ppermute(head, axis, [((i + 1) % count, i) for i in range(ends)]),
            ],
            axis=dim,
        )
    return cells


def unfold(padded, frames, height, breadth):
    pieces = []
    for shift_time in range(3):
        for shift_row in range(3):
            for shift_col in range(3):
                pieces.append(
                    padded[
                        shift_time : shift_time + frames,
                        shift_row : shift_row + height,
                        shift_col : shift_col + breadth,
                        :,
                    ]
                )
    return jnp.concatenate(pieces, axis=-1)


def norm_apply(upsampled, mean_chan, scale_chan, gain, bias):
    scaled = (upsampled.astype(jnp.float32) - mean_chan) * scale_chan
    return jax.nn.silu(scaled * gain + bias).astype(jnp.bfloat16)


def on_device(
    latent,
    cache_mid,
    norm1_gain,
    norm1_bias,
    conv1_weight,
    conv1_bias,
    cache_up,
    norm2_gain,
    norm2_bias,
    conv2_weight,
    conv2_bias,
):
    frames, height, breadth, chan_here = latent.shape
    groups_here = chan_here // GS
    values = latent.astype(jnp.float32)
    grouped = values.reshape(frames, height, breadth, groups_here, GS)
    entries = frames * height * lax.axis_size("space") * breadth * GS
    group_mean = lax.psum(jnp.sum(grouped, axis=(0, 1, 2, 4)), "space") / entries
    centred = grouped - group_mean[:, None]
    group_var = lax.psum(jnp.sum(centred * centred, axis=(0, 1, 2, 4)), "space") / entries
    scaled = (centred * lax.rsqrt(group_var + epsilon)[:, None]).reshape(
        frames, height, breadth, chan_here
    )
    normed_mid = jax.nn.silu(scaled * norm1_gain + norm1_bias).astype(jnp.bfloat16)
    joined = jnp.concatenate([cache_mid, normed_mid], axis=0)
    rimmed = extended(joined, (("space", 1),), 1)
    padded = jnp.pad(rimmed, ((0, 0), (0, 0), (1, 1), (0, 0)))
    columns = unfold(padded, frames, height, breadth).reshape(frames * height * breadth, -1)
    kernel = conv1_weight.reshape(-1, conv1_weight.shape[-1])
    summed = lax.psum_scatter(
        lax.dot_general(
            kernel, columns, (((0,), (1,)), ((), ())), preferred_element_type=jnp.float32
        ),
        "chan",
        scatter_dimension=0,
        tiled=True,
    )
    conv_mid = summed.T.reshape(frames, height, breadth, chan_here)
    merged = (values + conv_mid + conv1_bias).astype(jnp.bfloat16)
    merged_groups = merged.astype(jnp.float32).reshape(frames, height, breadth, groups_here, GS)
    first_group = lax.axis_index("chan") * groups_here

    def place(partial_value):
        return lax.dynamic_update_slice_in_dim(
            jnp.zeros((GROUPS,), jnp.float32), partial_value, first_group, 0
        )

    own_sum = jnp.sum(merged_groups, axis=(0, 1, 2, 4))
    group_sums, group_squares = lax.psum(
        (place(own_sum), place(jnp.sum(merged_groups * merged_groups, axis=(0, 1, 2, 4)))),
        ("space", "chan"),
    )
    up_mean = group_sums / entries
    up_var = group_squares / entries - up_mean * up_mean
    mean_chan = jnp.repeat(up_mean, GS)
    scale_chan = jnp.repeat(lax.rsqrt(up_var + epsilon), GS)
    pixel_tile = lax.all_to_all(merged, "chan", split_axis=2, concat_axis=3, tiled=True)
    upsampled = jnp.repeat(jnp.repeat(pixel_tile, 2, axis=1), 2, axis=2)
    normed_up = norm_apply(upsampled, mean_chan, scale_chan, norm2_gain, norm2_bias)
    joined_up = jnp.concatenate([cache_up, normed_up], axis=0)
    rimmed_up = extended(joined_up, (("space", 1), ("chan", 2)), 1)
    up_height = normed_up.shape[1]
    up_breadth = normed_up.shape[2]
    up_columns = unfold(rimmed_up, frames, up_height, up_breadth).reshape(
        frames * up_height * up_breadth, -1
    )
    kernel_up = conv2_weight.reshape(-1, conv2_weight.shape[-1])
    up_conv = jnp.dot(
        up_columns,
        lax.all_gather(kernel_up, "chan", axis=1, tiled=True),
        preferred_element_type=jnp.float32,
    )
    result = (up_conv + conv2_bias).astype(jnp.bfloat16).reshape(frames, up_height, up_breadth, -1)
    return result


MESH = pl.DeviceIdType.MESH
F32 = jnp.float32
BF16 = jnp.bfloat16


def group_total(row):
    lane = lax.broadcasted_iota(jnp.int32, row.shape, 1)
    width = row.shape[1]
    step = 1
    while step < GS:
        upper = pltpu.roll(row, width - step, 1)
        lower = pltpu.roll(row, step, 1)
        row = row + jnp.where(lane % (2 * step) < step, upper, lower)
        step *= 2
    return row


def local_stats(values):
    count = values.shape[0] * GS
    mean = group_total(jnp.sum(values, axis=0, keepdims=True)) / count
    centred = values - mean
    return mean, group_total(jnp.sum(centred * centred, axis=0, keepdims=True))


def whole_stats(stats_ref, count):
    parts = stats_ref.shape[0]
    means = stats_ref[:, 0:1, :]
    mean = jnp.sum(means, axis=0) / parts
    apart = means - mean[None]
    spread = jnp.sum(stats_ref[:, 1:2, :], axis=0) + count * jnp.sum(apart * apart, axis=0)
    return mean, lax.rsqrt(spread / (count * parts) + epsilon)


def norm_silu(values, mean, scale, gain, bias):
    moved = (values - mean) * scale * gain + bias
    shrunk = jnp.exp(-jnp.abs(moved))
    return (moved * jnp.where(moved < 0, shrunk, 1.0) / (1.0 + shrunk)).astype(BF16)


def from_left(values):
    place = lax.broadcasted_iota(jnp.int32, values.shape, 0)
    return jnp.where(place == 0, 0.0, pltpu.roll(values, 1, 0))


def from_right(values):
    size = values.shape[0]
    place = lax.broadcasted_iota(jnp.int32, values.shape, 0)
    return jnp.where(place == size - 1, 0.0, pltpu.roll(values, size - 1, 0))


def dot(a, b):
    return jnp.dot(a, b, preferred_element_type=F32)


def decoder_kernel(
    rows,
    chans,
    latent_hbm,
    cache_mid_hbm,
    gain1_hbm,
    bias1_hbm,
    w1_hbm,
    conv1_bias_hbm,
    cache_up,
    gain2_hbm,
    bias2_hbm,
    w2_hbm,
    conv2_bias_hbm,
    out,
    latent,
    cache_mid,
    gain1,
    bias1,
    conv1_bias,
    gain2,
    bias2,
    conv2_bias,
    w1,
    w2,
    halo_mid,
    stats1,
    stats2,
    part,
    summands,
    gathered,
    taps,
    rim_sum,
    rim_out,
    rim_in,
    normed,
    final,
    raised,
    upper_cells,
    lower_cells,
    above_cells,
    below_cells,
    out_send,
    out_recv,
    load_sem,
    halo_send,
    halo_recv,
    stat_send,
    stat_recv,
    sum_send,
    sum_recv,
    cache_send,
    cache_recv,
    rim_send,
    rim_recv,
    norm_send,
    norm_recv,
    last_send,
    last_recv,
):
    breadth, chan_here = latent.shape
    r = lax.axis_index("space")
    c = lax.axis_index("chan")
    has = (r > 0, r < rows - 1)
    beside = (r - 1, r + 1)
    mate = c + 1 - 2 * (c % 2)
    across = (c + 2) % chans

    def remote(src, dst, send, recv, **where):
        return pltpu.make_async_remote_copy(
            src_ref=src,
            dst_ref=dst,
            send_sem=send,
            recv_sem=recv,
            device_id=where,
            device_id_type=MESH,
        )

    moves = (
        (latent_hbm, latent),
        (w1_hbm, w1),
        (cache_mid_hbm, cache_mid),
        (gain1_hbm, gain1),
        (bias1_hbm, bias1),
        (conv1_bias_hbm, conv1_bias),
        (gain2_hbm, gain2),
        (bias2_hbm, bias2),
        (conv2_bias_hbm, conv2_bias),
        (cache_up, gathered.at[c]),
        (w2_hbm, w2),
    )
    loads = [
        pltpu.make_async_copy(source, target, load_sem.at[index])
        for index, (source, target) in enumerate(moves)
    ]
    for load in loads:
        load.start()

    barrier = pltpu.get_barrier_semaphore()
    for k in range(1, rows):
        pl.semaphore_signal(
            barrier, inc=1, device_id={"space": (r + k) % rows}, device_id_type=MESH
        )
    for k in range(1, chans):
        pl.semaphore_signal(
            barrier, inc=1, device_id={"chan": (c + k) % chans}, device_id_type=MESH
        )
    loads[0].wait()
    values = latent[...].astype(F32)
    mean, spread = local_stats(values)
    stats1[0, 0:1, :] = mean
    stats1[0, 1:2, :] = spread
    taps[...] = jnp.zeros_like(taps)
    for side in range(2):

        @pl.when(jnp.logical_not(has[side]))
        def _():
            halo_mid[side] = jnp.zeros(halo_mid.shape[1:], BF16)
            rim_in[side] = jnp.zeros(rim_in.shape[1:], BF16)

    pl.semaphore_wait(barrier, rows - 1 + chans - 1)

    def share(stats, which):
        copies = []
        for k in range(1, rows):
            copy = remote(
                stats.at[0],
                stats.at[k],
                stat_send.at[which, k],
                stat_recv.at[which, k],
                space=(r + k) % rows,
            )
            copy.start()
            copies.append(copy)
        return copies

    first_stats = share(stats1, 0)

    def halo_copies(side):
        return (
            remote(
                cache_mid_hbm,
                halo_mid.at[1 - side, pl.ds(0, 2)],
                halo_send.at[side, 0],
                halo_recv.at[1 - side, 0],
                space=beside[side],
            ),
            remote(
                latent_hbm,
                halo_mid.at[1 - side, 2],
                halo_send.at[side, 1],
                halo_recv.at[1 - side, 1],
                space=beside[side],
            ),
        )

    def halo_arrivals(side):
        return (
            remote(
                cache_mid_hbm,
                halo_mid.at[side, pl.ds(0, 2)],
                halo_send.at[side, 0],
                halo_recv.at[side, 0],
                space=beside[side],
            ),
            remote(
                latent_hbm,
                halo_mid.at[side, 2],
                halo_send.at[side, 1],
                halo_recv.at[side, 1],
                space=beside[side],
            ),
        )

    for side in range(2):

        @pl.when(has[side])
        def _():
            for copy in halo_copies(side):
                copy.start()

    own_across = remote(
        cache_up, gathered.at[c], cache_send.at[0], cache_recv.at[0], chan=across
    )
    own_mate = remote(cache_up, gathered.at[c], cache_send.at[1], cache_recv.at[1], chan=mate)
    passed = remote(
        gathered.at[across], gathered.at[across], cache_send.at[2], cache_recv.at[2], chan=mate
    )
    own_across.start()
    own_mate.start()
    for load in loads[1:-1]:
        load.wait()

    for side in range(2):

        @pl.when(has[side])
        def _():
            for copy in halo_arrivals(side):
                copy.wait_recv()

    def mid_taps(pieces, frames):
        cells = jnp.concatenate(pieces, axis=1)
        products = []
        for dx in range(3):
            weights = w1[frames, :, dx].reshape(cells.shape[1], w1.shape[-1])
            products.append(dot(cells, weights))
        return from_left(products[0]) + products[1] + from_right(products[2])

    pieces = []
    for frame in range(2):
        pieces += [halo_mid[0, frame], cache_mid[frame], halo_mid[1, frame]]
    cached_mid = mid_taps(pieces, slice(0, 2))

    for copy in first_stats:
        copy.wait_recv()
    mean, scale = whole_stats(stats1, breadth * GS)
    pieces = []
    for side in range(2):
        rim = norm_silu(halo_mid[side, 2].astype(F32), mean, scale, gain1[...], bias1[...])
        pieces.append(jnp.where(has[side], rim.astype(F32), 0.0).astype(BF16))
    pieces.insert(1, norm_silu(values, mean, scale, gain1[...], bias1[...]))
    partial = cached_mid + mid_taps(pieces, slice(2, 3))
    for block in range(chans):
        part[block] = partial[:, block * chan_here : (block + 1) * chan_here]
    sums = []
    for k in (2, 3, 1):
        to = (c + k) % chans
        copy = remote(part.at[to], summands.at[c], sum_send.at[k], sum_recv.at[k], chan=to)
        copy.start()
        sums.append(copy)
    summands[c] = part[c]

    def up_taps(base):
        def step(index, _):
            frame = index // 3
            dy = index % 3
            cells = gathered[pl.ds(base, 2), frame]
            cells = cells.reshape(-1, cells.shape[-1])
            weights = jnp.concatenate([w2[frame, dy, dx] for dx in range(3)], axis=1)
            product = dot(cells, weights).reshape((2, 2) + taps.shape[2:])
            for row in range(2):
                taps[row + 2 - dy, pl.ds(base, 2)] += product[:, row]
            return 0

        lax.fori_loop(0, 6, step, 0)

    base = c - c % 2
    loads[-1].wait()
    own_mate.wait_recv()
    up_taps(base)
    own_across.wait_recv()
    passed.start()

    for copy in sums:
        copy.wait_recv()
    conv_mid = summands[0]
    for block in range(1, chans):
        conv_mid = conv_mid + summands[block]
    merged = (values + conv_mid + conv1_bias[...]).astype(BF16).astype(F32)
    mean, spread = local_stats(merged)
    stats2[0, 0:1, :] = mean
    stats2[0, 1:2, :] = spread
    second_stats = share(stats2, 1)

    passed.wait_recv()
    up_taps((base + 2) % chans)

    def combined(row):
        cells = taps[row].reshape(-1, taps.shape[-1])
        lanes = [cells[:, dx * chan_here : (dx + 1) * chan_here] for dx in range(3)]
        return from_left(lanes[0]) + lanes[1] + from_right(lanes[2])

    for side in range(2):
        rim_sum[side] = combined(3 * side)
        final[side] = combined(1 + side) + conv2_bias[c]

    for copy in second_stats:
        copy.wait_recv()
    mean, scale = whole_stats(stats2, breadth * GS)
    normed[c] = norm_silu(merged, mean, scale, gain2[c], bias2[c])

    def rim_copy(side):
        return remote(
            rim_out.at[side],
            rim_in.at[1 - side],
            rim_send.at[side],
            rim_recv.at[1 - side],
            space=beside[side],
        )

    def rim_arrival(side):
        return remote(
            rim_out.at[side],
            rim_in.at[side],
            rim_send.at[side],
            rim_recv.at[side],
            space=beside[side],
        )

    along = []
    for k in (2, 3, 1):
        copy = remote(
            normed.at[c], normed.at[c], norm_send.at[k], norm_recv.at[k], chan=(c + k) % chans
        )
        copy.start()
        along.append(copy)

    def raise_taps(dy, _):
        cells = jnp.concatenate([normed[block] for block in range(chans)], axis=1)
        weights = jnp.concatenate([w2[2, dy, dx] for dx in range(3)], axis=1)
        raised[dy] = dot(cells, weights)
        return 0

    def weave(product, woven):
        lanes = [product[:, dx * chan_here : (dx + 1) * chan_here] for dx in range(3)]
        woven[pl.ds(0, breadth, stride=2), :] = from_left(lanes[0]) + lanes[1] + lanes[2]
        woven[pl.ds(1, breadth, stride=2), :] = lanes[0] + lanes[1] + from_right(lanes[2])

    for copy in along:
        copy.wait_recv()
    lax.fori_loop(0, 3, raise_taps, 0)
    for side, woven in enumerate((above_cells, below_cells)):
        weave(raised[2 * (1 - side)], woven)
        rim_out[side] = (rim_sum[side] + woven[...]).astype(BF16)

        @pl.when(has[side])
        def _():
            rim_copy(side).start()

    for row, woven in enumerate((upper_cells, lower_cells)):
        weave(raised[1] + raised[2 * (1 - row)], woven)
        final[row] += woven[...]

    for side in range(2):

        @pl.when(has[side])
        def _():
            rim_arrival(side).wait_recv()

    for row in range(2):
        result = (final[row] + rim_in[row].astype(F32)).astype(BF16)
        share_cols = out.shape[1]
        for block in range(chans):
            out_send[block, row] = result[block * share_cols : (block + 1) * share_cols]

    lasts = []
    for k in (2, 3, 1):
        to = (c + k) % chans
        copy = remote(out_send.at[to], out_recv.at[c], last_send.at[k], last_recv.at[k], chan=to)
        copy.start()
        lasts.append(copy)
    out_recv[c] = out_send[c]

    for copy in first_stats + second_stats + sums + along + [own_across, own_mate, passed]:
        copy.wait_send()
    for side in range(2):

        @pl.when(has[side])
        def _():
            for copy in halo_copies(side):
                copy.wait_send()
            rim_copy(side).wait_send()

    for copy in lasts:
        copy.wait_recv()
    for block in range(chans):
        out[:, :, block * chan_here : (block + 1) * chan_here] = out_recv[block]
    for copy in lasts:
        copy.wait_send()


def fused_on_device(
    rows,
    chans,
    latent,
    cache_mid,
    norm1_gain,
    norm1_bias,
    conv1_weight,
    conv1_bias,
    cache_up,
    norm2_gain,
    norm2_bias,
    conv2_weight,
    conv2_bias,
):
    breadth, chan_here = latent.shape[2:]
    up_rows, up_cols, chan_all = cache_up.shape[1:]
    vmem = pl.BlockSpec(memory_space=pltpu.VMEM)
    hbm = pl.BlockSpec(memory_space=pltpu.HBM)
    dma = pltpu.SemaphoreType.DMA
    result = pl.pallas_call(
        functools.partial(decoder_kernel, rows, chans),
        out_shape=jax.ShapeDtypeStruct((up_rows, up_cols, chan_all), BF16),
        in_specs=[hbm] * 11,
        out_specs=vmem,
        scratch_shapes=[
            pltpu.VMEM((breadth, chan_here), BF16),
            pltpu.VMEM((2, breadth, chan_here), BF16),
            pltpu.VMEM((1, chan_here), F32),
            pltpu.VMEM((1, chan_here), F32),
            pltpu.VMEM((1, chan_here), F32),
            pltpu.VMEM((chans, 1, chan_here), F32),
            pltpu.VMEM((chans, 1, chan_here), F32),
            pltpu.VMEM((chans, 1, chan_here), F32),
            pltpu.VMEM(conv1_weight.shape, BF16),
            pltpu.VMEM(conv2_weight.shape, BF16),
            pltpu.VMEM((2, 3, breadth, chan_here), BF16),
            pltpu.VMEM((rows, 8, chan_here), F32),
            pltpu.VMEM((rows, 8, chan_here), F32),
            pltpu.VMEM((chans, breadth, chan_here), F32),
            pltpu.VMEM((chans, breadth, chan_here), F32),
            pltpu.VMEM((chans,) + cache_up.shape, BF16),
            pltpu.VMEM((4, chans, up_cols, 3 * chan_here), F32),
            pltpu.VMEM((2, 2 * breadth, chan_here), F32),
            pltpu.VMEM((2, 2 * breadth, chan_here), BF16),
            pltpu.VMEM((2, 2 * breadth, chan_here), BF16),
            pltpu.VMEM((chans, breadth, chan_here), BF16),
            pltpu.VMEM((2, 2 * breadth, chan_here), F32),
            pltpu.VMEM((3, breadth, 3 * chan_here), F32),
            pltpu.VMEM((2 * breadth, chan_here), F32),
            pltpu.VMEM((2 * breadth, chan_here), F32),
            pltpu.VMEM((2 * breadth, chan_here), F32),
            pltpu.VMEM((2 * breadth, chan_here), F32),
            pltpu.VMEM((chans, up_rows, up_cols, chan_here), BF16),
            pltpu.VMEM((chans, up_rows, up_cols, chan_here), BF16),
            dma((11,)),
            dma((2, 2)),
            dma((2, 2)),
            dma((2, rows)),
            dma((2, rows)),
            dma((chans,)),
            dma((chans,)),
            dma((3,)),
            dma((3,)),
            dma((2,)),
            dma((2,)),
            dma((chans,)),
            dma((chans,)),
            dma((chans,)),
            dma((chans,)),
        ],
        compiler_params=pltpu.CompilerParams(
            collective_id=0, has_side_effects=True, vmem_limit_bytes=56 * 2**20
        ),
    )(
        latent[0, 0],
        cache_mid[:, 0],
        norm1_gain[None],
        norm1_bias[None],
        conv1_weight,
        conv1_bias[None],
        cache_up,
        norm2_gain.reshape(chans, 1, chan_here),
        norm2_bias.reshape(chans, 1, chan_here),
        conv2_weight,
        conv2_bias.reshape(chans, 1, chan_here),
    )
    return result[None]


def fits_kernel(
    rows, chans, latent, cache_up
):
    return (
        latent.shape[:2] == (1, 1)
        and cache_up.shape[:2] == (2, 2)
        and chans == 4
        and rows > 1
        and latent.shape[3] == 128
        and cache_up.shape[2] % 16 == 0
    )


def solution(mesh):
    placed = (
        P(None, "space", None, "chan"),
        P(None, "space", None, "chan"),
        P("chan"),
        P("chan"),
        P(None, None, None, "chan", None),
        P("chan"),
        P(None, "space", "chan", None),
        P(),
        P(),
        P(None, None, None, None, "chan"),
        P(),
    )
    rows = mesh.shape["space"]
    chans = mesh.shape["chan"]

    def one_device(*args):
        if fits_kernel(rows, chans, args[0], args[6]):
            return fused_on_device(rows, chans, *args)
        return on_device(*args)

    return jax.shard_map(
        one_device,
        mesh=mesh,
        in_specs=placed,
        out_specs=P(None, "space", "chan", None),
        check_vma=False,
    )
```
